32 devices in a mesh: dp: 4 (over x, core), mp: 8 (over z, y).
Axes of the slice: x: 2, y: 2, z: 4, core: 2. Of those that a mesh axis runs over, the one named last changes fastest.
Arguments:
- residual_input: bfloat16 [2048, 4608], P(('dp', 'mp')), may hold values from -6 to 6
- before_attention_gain: float32 [4608], replicated, may hold values from 0.25 to 1.75
- after_attention_gain: float32 [4608], replicated, may hold values from 0.25 to 1.75
- before_feedforward_gain: float32 [4608], replicated, may hold values from 0.25 to 1.75
- after_feedforward_gain: float32 [4608], replicated, may hold values from 0.25 to 1.75
- query_weight: bfloat16 [4608, 4096], P(None, 'mp'), may hold values from -0.09375 to 0.09375
- key_value_weight: bfloat16 [4608, 2, 32, 128], P(None, None, 'mp'), as said below
- output_weight: bfloat16 [4096, 4608], P('mp'), may hold values from -0.09375 to 0.09375
- gate_matrix: bfloat16 [4608, 20480], P(None, 'mp'), may hold values from -0.09375 to 0.09375
- up_matrix: bfloat16 [4608, 20480], P(None, 'mp'), may hold values from -0.09375 to 0.09375
- down_matrix: bfloat16 [20480, 4608], P('mp'), may hold values from -0.0390625 to 0.0390625
- key_value_cache: bfloat16 [256, 2, 32, 16, 128], P('dp', None, 'mp'), as said below
- projected_lowrank_left: bfloat16 [64, 4608, 16], P('mp'), may hold values from -0.09375 to 0.09375
- projected_lowrank_right: bfloat16 [64, 16, 3, 32, 128], P(None, None, None, 'mp'), as said below
- result_lowrank_left: bfloat16 [64, 4096, 16], P(None, 'mp'), may hold values from -0.09375 to 0.09375
- result_lowrank_right: bfloat16 [64, 16, 4608], P('mp'), may hold values from -1.5 to 1.5
- token_request: int32 [4, 512], P('dp'), may hold values from 0 to 7, never falling along the last dimension, each value on 1 to 256 neighbouring positions
- lowrank_choice_by_prompt: int32 [4, 8], P('dp'), may hold values from 0 to 63
- adapter_position: int32 [64], replicated, may hold values from 0 to 63, each once
- request_pages: int32 [4, 8, 4], replicated, may hold values from 0 to 255
Outputs:
- hidden_out: bfloat16 [2048, 4608], P(('dp', 'mp'))
- kv_new: bfloat16 [2048, 2, 32, 128], P('dp', None, 'mp')
The draws below stay inside these ranges and needn't reach their ends.
Inputs may be any that keep to these rules, and one draw needn't show every extreme that they name: `key_value_weight`: query heads h and h2 with h // 2 == h2 // 2 have equal key and value weights: they share one key and value head. `key_value_cache`: query heads that share a key and value head have equal cached keys and values. `projected_lowrank_right`: the key and value parts of query heads that share a key and value head are equal. `token_request`: numbers never fall along a group; every request has at least one token. `adapter_position`: each slot once. `request_pages`: pages may repeat within and across requests.
All inputs are finite; a program needn't handle non-finite values.
Results may differ from the reference program's by a relative error of at most 0.035.
Values may be sent and summed in bfloat16 or wider, within the bound.
A program may use at most 192 MiB of HBM per device.

```python
import math
import jax
import jax.numpy as jnp
import numpy as np
from jax import lax

HIDDEN_BREADTH = 4608
ASKING_CHANNELS = 32
PAIR_CHANNELS = 16
CHANNEL_LENGTH = 128
FF = 20480
NUM_LOW_TERMS = 64
LOW_DIMENSION = 16
SHARD_PROMPT_LEN = 512
SHARD_PROMPTS = 8
PPR = 4
PAGE = 16
PROMPT_LEN_ALL = 2048
POOL = 256
N_DP = 4
N_MP = 8


def common_channels(key, dims_shape, head_axis, spread):
    drawn = jax.random.normal(key, dims_shape, jnp.float32) * spread
    return jnp.repeat(drawn, ASKING_CHANNELS // PAIR_CHANNELS, axis=head_axis)


def draw_key_value_weight(key, part):
    return common_channels(jax.random.fold_in(key, 11), (HIDDEN_BREADTH, 2, PAIR_CHANNELS, CHANNEL_LENGTH), 2, HIDDEN_BREADTH ** (-0.5)).astype(jnp.bfloat16)


def draw_key_value_cache(key, part):
    return common_channels(jax.random.fold_in(key, 12), (POOL, 2, PAIR_CHANNELS, PAGE, CHANNEL_LENGTH), 2, 1.0).astype(jnp.bfloat16)


def draw_projected_lowrank_right(key, part):
    asking_share = jax.random.normal(jax.random.fold_in(key, 13), (NUM_LOW_TERMS, LOW_DIMENSION, 1, ASKING_CHANNELS, CHANNEL_LENGTH), jnp.float32) * LOW_DIMENSION ** (-0.5)
    common_share = common_channels(jax.random.fold_in(key, 14), (NUM_LOW_TERMS, LOW_DIMENSION, 2, PAIR_CHANNELS, CHANNEL_LENGTH), 3, LOW_DIMENSION ** (-0.5))
    return jnp.concatenate([asking_share, common_share], axis=2).astype(jnp.bfloat16)


def touch_ends(values, own_key, least, high):
    spot = [jax.random.randint(jax.random.fold_in(own_key, axis), (), 0, length) for axis, length in enumerate(values.shape)]
    main_axis = values.shape.index(max(values.shape))
    beside = spot[:main_axis] + [(spot[main_axis] + 1) % values.shape[main_axis]] + spot[main_axis + 1:]
    return values.at[tuple(spot)].set(least).at[tuple(beside)].set(high)


def level_of(stream_key, dims, shards, smallest, top_value):
    level, own = 1.0, jax.random.fold_in(stream_key, 6)
    for axis_at, parts in shards:
        heights = jnp.exp(jax.random.uniform(jax.random.fold_in(own, axis_at), (parts,), jnp.float32, smallest / len(shards), top_value / len(shards)))
        level = level * jnp.repeat(heights, dims[axis_at] // parts).reshape([-1 if axis == axis_at else 1 for axis in range(len(dims))])
    return level


def cumulative_ranks(amount, lean):
    portions = [(1 << 20) // math.isqrt(rank ** lean) + 1 for rank in range(1, amount + 1)]
    width = 1 + sum(portions) // (1 << 30)
    return np.cumsum(np.array([max(1, weight // width) for weight in portions]))


def ranked(own_key, shape, count, skew):
    listing = cumulative_ranks(count, skew)
    ticket = jax.random.randint(jax.random.fold_in(own_key, 1), shape, 0, int(listing[count - 1]))
    standing = jnp.searchsorted(jnp.asarray(listing, jnp.int32), ticket, side="right")
    return jax.random.permutation(jax.random.fold_in(own_key, 2), count)[standing].astype(jnp.int32)


def split_up(count, total, limit, slope):
    weights = [(1 << 20) // math.isqrt(standing ** slope) + 1 for standing in range(2, count + 1)]
    spare, holding = total - limit - (count - 1), [1] * (count - 1)
    while spare > 0:
        candidates = [i for i in range(count - 1) if holding[i] < limit]
        whole, budget = sum([weights[i] for i in candidates]), spare
        for i in candidates:
            more = min(limit - holding[i], max(1, budget * weights[i] // whole), spare)
            holding[i] = holding[i] + more
            spare = spare - more
    return np.array([limit] + holding)


def uneven(own_key, number_of, total, reach, skew):
    if number_of == 2:
        one = jax.random.randint(own_key, (), max(1, total - reach), min(reach, total - 1) + 1)
        return jnp.stack([one, total - one])
    sizes = jnp.asarray(split_up(number_of, total, reach, skew), jnp.int32)
    couples = (number_of - 1) // 2
    donor, taker = sizes[1:1 + 2 * couples:2], sizes[2:2 + 2 * couples:2]
    room = jnp.minimum(donor - 1, reach - taker)
    shifted = jax.random.randint(jax.random.fold_in(own_key, 1), (couples,), 0, 1 << 20) % (room + 1)
    sizes = sizes.at[1:1 + 2 * couples:2].set(donor - shifted).at[2:2 + 2 * couples:2].set(taker + shifted)
    return sizes[jax.random.permutation(jax.random.fold_in(own_key, 2), number_of)]


def gaussian(key, extent, scale, bound, split=(), held_as=jnp.bfloat16):
    array = scale * jax.random.normal(key, extent, jnp.float32)
    if split:
        array = array * level_of(key, extent, split, -0.22, 0.18)
    return jnp.clip(array, -bound, bound).astype(held_as)


def setup_inputs(seed: int = 0) -> dict:
    key_of = jax.random.split(jax.random.key(seed), 21)
    residual_input = gaussian(key_of[0], (PROMPT_LEN_ALL, HIDDEN_BREADTH), 1.0, 6.0, ((0, 32),))
    before_attention_gain = jnp.clip(1.0 + 0.15 * jax.random.normal(key_of[1], (HIDDEN_BREADTH,), jnp.float32), 0.25, 1.75)
    after_attention_gain = jnp.clip(1.0 + 0.15 * jax.random.normal(key_of[2], (HIDDEN_BREADTH,), jnp.float32), 0.25, 1.75)
    before_feedforward_gain = jnp.clip(1.0 + 0.15 * jax.random.normal(key_of[3], (HIDDEN_BREADTH,), jnp.float32), 0.25, 1.75)
    after_feedforward_gain = jnp.clip(1.0 + 0.15 * jax.random.normal(key_of[4], (HIDDEN_BREADTH,), jnp.float32), 0.25, 1.75)
    query_weight = gaussian(key_of[5], (HIDDEN_BREADTH, ASKING_CHANNELS * CHANNEL_LENGTH), HIDDEN_BREADTH ** -0.5, 0.09375, ((1, 8),))
    key_value_weight = draw_key_value_weight(jax.random.fold_in(key_of[20], 71), 0)
    output_weight = gaussian(key_of[7], (ASKING_CHANNELS * CHANNEL_LENGTH, HIDDEN_BREADTH), (ASKING_CHANNELS * CHANNEL_LENGTH) ** -0.5, 0.09375, ((0, 8),))
    gate_matrix = gaussian(key_of[8], (HIDDEN_BREADTH, FF), HIDDEN_BREADTH ** -0.5, 0.09375, ((1, 8),))
    up_matrix = gaussian(key_of[9], (HIDDEN_BREADTH, FF), HIDDEN_BREADTH ** -0.5, 0.09375, ((1, 8),))
    down_matrix = gaussian(key_of[10], (FF, HIDDEN_BREADTH), FF ** -0.5, 0.0390625, ((0, 8),))
    key_value_cache = draw_key_value_cache(jax.random.fold_in(key_of[20], 71), 0)
    projected_lowrank_left = gaussian(key_of[12], (NUM_LOW_TERMS, HIDDEN_BREADTH, LOW_DIMENSION), HIDDEN_BREADTH ** -0.5, 0.09375, ((0, 8),))
    projected_lowrank_right = draw_projected_lowrank_right(jax.random.fold_in(key_of[20], 71), 0)
    result_lowrank_left = gaussian(key_of[14], (NUM_LOW_TERMS, ASKING_CHANNELS * CHANNEL_LENGTH, LOW_DIMENSION), (ASKING_CHANNELS * CHANNEL_LENGTH) ** -0.5, 0.09375, ((1, 8),))
    result_lowrank_right = gaussian(key_of[15], (NUM_LOW_TERMS, LOW_DIMENSION, HIDDEN_BREADTH), LOW_DIMENSION ** -0.5, 1.5, ((0, 8),))
    token_request = jax.vmap(lambda own: jnp.searchsorted(jnp.cumsum(uneven(own, SHARD_PROMPTS, SHARD_PROMPT_LEN, SHARD_PROMPT_LEN // 2, 2)), jnp.arange(SHARD_PROMPT_LEN), side="right"))(jax.random.split(key_of[16], N_DP)).reshape((N_DP, SHARD_PROMPT_LEN)).astype(jnp.int32)
    lowrank_choice_by_prompt = touch_ends(ranked(key_of[17], (N_DP, SHARD_PROMPTS), NUM_LOW_TERMS, 2), jax.random.fold_in(key_of[17], 3), 0, NUM_LOW_TERMS - 1).astype(jnp.int32)
    adapter_position = jax.random.permutation(key_of[18], NUM_LOW_TERMS).astype(jnp.int32)
    request_pages = touch_ends(jax.random.randint(key_of[19], (N_DP, SHARD_PROMPTS, PPR), 0, POOL), jax.random.fold_in(key_of[19], 1), 0, POOL - 1).astype(jnp.int32)
    return {"residual_input": residual_input, "before_attention_gain": before_attention_gain, "after_attention_gain": after_attention_gain, "before_feedforward_gain": before_feedforward_gain, "after_feedforward_gain": after_feedforward_gain, "query_weight": query_weight, "key_value_weight": key_value_weight, "output_weight": output_weight, "gate_matrix": gate_matrix, "up_matrix": up_matrix, "down_matrix": down_matrix, "key_value_cache": key_value_cache, "projected_lowrank_left": projected_lowrank_left, "projected_lowrank_right": projected_lowrank_right, "result_lowrank_left": result_lowrank_left, "result_lowrank_right": result_lowrank_right, "token_request": token_request, "lowrank_choice_by_prompt": lowrank_choice_by_prompt, "adapter_position": adapter_position, "request_pages": request_pages}


EPS = 1e-06
SOFTCAP = 50.0

def rms_scale(values, scaling):
    mean_square = lax.optimization_barrier(jnp.mean(values * values, axis=-1, keepdims=True))
    return values * lax.rsqrt(mean_square + EPS) * scaling.astype(jnp.float32)

def apply_rotary(values, token_positions):
    half_dim = values.shape[-1] // 2
    frequency = 10000.0 ** (-2.0 * jnp.arange(half_dim, dtype=jnp.float32) / values.shape[-1])
    angles = token_positions.astype(jnp.float32)[:, None] * frequency[None, :]
    cosine = jnp.cos(angles)[:, None, :]
    sine_part = jnp.sin(angles)[:, None, :]
    first_half = values[..., :half_dim]
    second_half = values[..., half_dim:]
    return jnp.concatenate([first_half * cosine - second_half * sine_part, second_half * cosine + first_half * sine_part], axis=-1)

def positions_of(segments):
    length = segments.shape[0]
    earlier = lax.optimization_barrier(jnp.sum((segments[None, :] < segments[:, None]).astype(jnp.int32), axis=1))
    return (PPR * PAGE + jnp.arange(length, dtype=jnp.int32) - earlier).astype(jnp.int32)

def capped(scores):
    return SOFTCAP * jnp.tanh(scores / SOFTCAP)

def attend(query_rows, keys_new, fresh_values, keys_pre, values_pre, segments):
    scale_factor = 1.0 / math.sqrt(HIDDEN_BREADTH // ASKING_CHANNELS)
    length = segments.shape[0]
    prefix_owner = jnp.arange(keys_pre.shape[1], dtype=jnp.int32) // (PPR * PAGE)
    mask_pre = (prefix_owner[None, :] == segments[:, None])[None]
    ordinal = jnp.arange(length, dtype=jnp.int32)
    mask_new = ((segments[None, :] == segments[:, None]) & (ordinal[None, :] <= ordinal[:, None]))[None]
    scores_pre = jnp.einsum('thd,hjd->htj', query_rows.astype(jnp.float32), keys_pre.astype(jnp.float32)) * scale_factor
    scores_new = jnp.einsum('thd,uhd->htu', query_rows.astype(jnp.float32), keys_new.astype(jnp.float32)) * scale_factor
    weight_pre = jnp.where(mask_pre, jnp.exp(capped(scores_pre)), 0.0)
    weight_new = jnp.where(mask_new, jnp.exp(capped(scores_new)), 0.0)
    totals = lax.optimization_barrier(jnp.sum(weight_pre, axis=-1, keepdims=True)) + lax.optimization_barrier(jnp.sum(weight_new, axis=-1, keepdims=True))
    probs_pre = (weight_pre / totals).astype(jnp.bfloat16)
    probs_new = (weight_new / totals).astype(jnp.bfloat16)
    mixture = jnp.einsum('htj,hjd->thd', probs_pre.astype(jnp.float32), values_pre.astype(jnp.float32))
    mixture = mixture + jnp.einsum('htu,uhd->thd', probs_new.astype(jnp.float32), fresh_values.astype(jnp.float32))
    return mixture.astype(jnp.bfloat16).reshape(length, -1)

def reference(residual_input, before_attention_gain, after_attention_gain, before_feedforward_gain, after_feedforward_gain, query_weight, key_value_weight, output_weight, gate_matrix, up_matrix, down_matrix, key_value_cache, projected_lowrank_left, projected_lowrank_right, result_lowrank_left, result_lowrank_right, token_request, lowrank_choice_by_prompt, adapter_position, request_pages):
    residual = residual_input.astype(jnp.float32)
    normalized_rows = rms_scale(residual, before_attention_gain).astype(jnp.bfloat16)
    query_rows = jnp.dot(normalized_rows, query_weight, preferred_element_type=jnp.float32).reshape(PROMPT_LEN_ALL, ASKING_CHANNELS, CHANNEL_LENGTH)
    key_value_rows = jnp.dot(normalized_rows, key_value_weight.reshape(HIDDEN_BREADTH, 2 * ASKING_CHANNELS * CHANNEL_LENGTH), preferred_element_type=jnp.float32).reshape(PROMPT_LEN_ALL, 2, ASKING_CHANNELS, CHANNEL_LENGTH)
    group_of = (jnp.arange(PROMPT_LEN_ALL, dtype=jnp.int32) // SHARD_PROMPT_LEN).astype(jnp.int32)
    flat_segments = token_request.reshape(PROMPT_LEN_ALL)
    token_adapter = lowrank_choice_by_prompt[group_of, flat_segments]
    token_adapter_slot = adapter_position[token_adapter]
    gathered_down = jnp.einsum('bg,wgv->bwv', normalized_rows.astype(jnp.float32), projected_lowrank_left.astype(jnp.float32))
    lowrank_source = jnp.take_along_axis(gathered_down, token_adapter_slot[:, None, None].astype(jnp.int32), axis=1)[:, 0, :].astype(jnp.bfloat16)
    request_range = jnp.arange(SHARD_PROMPTS, dtype=jnp.int32)
    adapter_pieces = []
    position_parts = []
    for shard_ordinal in range(N_DP):
        line_span = slice(shard_ordinal * SHARD_PROMPT_LEN, (shard_ordinal + 1) * SHARD_PROMPT_LEN)
        segments = token_request[shard_ordinal]
        choice_mask_table = (segments[:, None] == request_range[None, :]).astype(jnp.bfloat16)
        broadened_lines = (choice_mask_table[:, :, None] * lowrank_source[line_span][:, None, :]).reshape(SHARD_PROMPT_LEN, SHARD_PROMPTS * LOW_DIMENSION)
        raised_result_lines = projected_lowrank_right[lowrank_choice_by_prompt[shard_ordinal]].reshape(SHARD_PROMPTS * LOW_DIMENSION, 3 * ASKING_CHANNELS * CHANNEL_LENGTH)
        adapter_pieces.append(jnp.dot(broadened_lines, raised_result_lines, preferred_element_type=jnp.float32))
        position_parts.append(positions_of(segments))
    adapter_query_key_value = jnp.concatenate(adapter_pieces, axis=0).reshape(PROMPT_LEN_ALL, 3, ASKING_CHANNELS, CHANNEL_LENGTH)
    token_positions = jnp.concatenate(position_parts, axis=0)
    rotary_queries = apply_rotary(query_rows + adapter_query_key_value[:, 0], token_positions).astype(jnp.bfloat16)
    rotary_keys = apply_rotary(key_value_rows[:, 0] + adapter_query_key_value[:, 1], token_positions).astype(jnp.bfloat16)
    fresh_values = (key_value_rows[:, 1] + adapter_query_key_value[:, 2]).astype(jnp.bfloat16)
    kv_new = jnp.stack([rotary_keys, fresh_values], axis=1)
    attended_parts = []
    output_adapter_pieces = []
    for shard_ordinal in range(N_DP):
        line_span = slice(shard_ordinal * SHARD_PROMPT_LEN, (shard_ordinal + 1) * SHARD_PROMPT_LEN)
        segments = token_request[shard_ordinal]
        page_ids = request_pages[shard_ordinal].reshape(SHARD_PROMPTS * PPR)
        chosen = key_value_cache[page_ids]
        keys_pre = jnp.transpose(chosen[:, 0], (1, 0, 2, 3)).reshape(ASKING_CHANNELS, SHARD_PROMPTS * PPR * PAGE, CHANNEL_LENGTH)
        values_pre = jnp.transpose(chosen[:, 1], (1, 0, 2, 3)).reshape(ASKING_CHANNELS, SHARD_PROMPTS * PPR * PAGE, CHANNEL_LENGTH)
        attended = attend(rotary_queries[line_span], rotary_keys[line_span], fresh_values[line_span], keys_pre, values_pre, segments)
        attended_parts.append(attended)
        membership = segments[:, None] == request_range[None, :]
        down_output_rows = result_lowrank_left[lowrank_choice_by_prompt[shard_ordinal]]
        request_factors = jnp.einsum('tc,rck->trk', attended.astype(jnp.float32), down_output_rows.astype(jnp.float32))
        output_adapter_pieces.append(lax.optimization_barrier(jnp.sum(jnp.where(membership[:, :, None], request_factors, 0.0), axis=1)))
    attended_all = jnp.concatenate(attended_parts, axis=0)
    result_lowrank_source = jnp.concatenate(output_adapter_pieces, axis=0).astype(jnp.bfloat16)
    cols_dev = ASKING_CHANNELS * CHANNEL_LENGTH // N_MP
    seats_each_shard = NUM_LOW_TERMS // N_MP
    units_dev = FF // N_MP

    def attn_shard(shard_place, running):
        start_col = (shard_place * cols_dev).astype(jnp.int32)
        attn_part = lax.dynamic_slice_in_dim(attended_all, start_col, cols_dev, 1)
        weight_part = lax.dynamic_slice_in_dim(output_weight, start_col, cols_dev, 0)
        slot_ids = (shard_place * seats_each_shard + jnp.arange(seats_each_shard, dtype=jnp.int32)).astype(jnp.int32)
        resident_here = (token_adapter_slot[:, None] == slot_ids[None, :]).astype(jnp.bfloat16)
        broadened_result = (resident_here[:, :, None] * result_lowrank_source[:, None, :]).reshape(PROMPT_LEN_ALL, seats_each_shard * LOW_DIMENSION)
        raised_fragment = lax.dynamic_slice_in_dim(result_lowrank_right, (shard_place * seats_each_shard).astype(jnp.int32), seats_each_shard, 0).reshape(seats_each_shard * LOW_DIMENSION, HIDDEN_BREADTH)
        shard_sum = jnp.dot(attn_part, weight_part, preferred_element_type=jnp.float32) + jnp.dot(broadened_result, raised_fragment, preferred_element_type=jnp.float32)
        return running + lax.optimization_barrier(shard_sum.astype(jnp.bfloat16)).astype(jnp.float32)
    attn_sum = lax.fori_loop(jnp.int32(0), jnp.int32(N_MP), attn_shard, jnp.zeros((PROMPT_LEN_ALL, HIDDEN_BREADTH), jnp.float32))
    after_attn = (residual + rms_scale(attn_sum, after_attention_gain)).astype(jnp.bfloat16)
    normed_ffw = rms_scale(after_attn.astype(jnp.float32), before_feedforward_gain).astype(jnp.bfloat16)
    gated = jnp.dot(normed_ffw, gate_matrix, preferred_element_type=jnp.float32)
    upward = jnp.dot(normed_ffw, up_matrix, preferred_element_type=jnp.float32)
    hidden = (jax.nn.gelu(gated, approximate=True) * upward).astype(jnp.bfloat16)

    def ffw_shard(shard_place, running):
        start_unit = (shard_place * units_dev).astype(jnp.int32)
        hidden_part = lax.dynamic_slice_in_dim(hidden, start_unit, units_dev, 1)
        down_part = lax.dynamic_slice_in_dim(down_matrix, start_unit, units_dev, 0)
        shard_sum = jnp.dot(hidden_part, down_part, preferred_element_type=jnp.float32)
        return running + lax.optimization_barrier(shard_sum.astype(jnp.bfloat16)).astype(jnp.float32)
    ffw_sum = lax.fori_loop(jnp.int32(0), jnp.int32(N_MP), ffw_shard, jnp.zeros((PROMPT_LEN_ALL, HIDDEN_BREADTH), jnp.float32))
    hidden_out = (after_attn.astype(jnp.float32) + rms_scale(ffw_sum, after_feedforward_gain)).astype(jnp.bfloat16)
    return (hidden_out, kv_new)
```

```python
import functools
import math

import jax
import jax.numpy as jnp
from jax import lax
from jax.experimental import pallas as pl
from jax.experimental.pallas import tpu as pltpu
from jax.sharding import PartitionSpec as P

HIDDEN_BREADTH = 4608
ASKING_CHANNELS = 32
CHANNEL_LENGTH = 128
NUM_LOW_TERMS = 64
LOW_DIMENSION = 16
SHARD_PROMPTS = 8
PPR = 4
PAGE = 16


EPS = 1e-06
SOFTCAP = 50.0
MESH = pl.DeviceIdType.MESH
ANY = pl.BlockSpec(memory_space=pl.ANY)
VMEM = pl.BlockSpec(memory_space=pltpu.VMEM)
SMEM = pl.BlockSpec(memory_space=pltpu.SMEM)


def ring_place(index, n):
    return jnp.where(index % 2 == 0, index // 2, n - 1 - index // 2)


def ring_index(place, n):
    place = lax.rem(place + 2 * n, n)
    return jnp.where(place < n // 2, 2 * place, 2 * (n - 1 - place) + 1)


def greet_neighbours(place, n):
    barrier = pltpu.get_barrier_semaphore()
    for way in (1, -1):
        pl.semaphore_signal(
            barrier, inc=1, device_id={"mp": ring_index(place + way, n)}, device_id_type=MESH
        )
    pl.semaphore_wait(barrier, 2)


SUB = 2


def gather_kernel(n, x_ref, out_ref, send_sem, recv_sem, own_sem):
    rows, cols = x_ref.shape
    width = cols // (2 * SUB)
    place = ring_place(lax.axis_index("mp"), n)
    greet_neighbours(place, n)

    def window(owner, lane):
        return out_ref.at[
            pl.ds(pl.multiple_of(owner * rows, rows), rows), pl.ds(lane * width, width)
        ]

    def copy(step, lane, first):
        way = 1 if lane < SUB else -1
        owner = ring_index(place - way * step, n)
        src = x_ref.at[:, pl.ds(lane * width, width)] if first else window(owner, lane)
        return pltpu.make_async_remote_copy(
            src_ref=src,
            dst_ref=window(owner, lane),
            send_sem=send_sem.at[lane, step],
            recv_sem=recv_sem.at[lane, step],
            device_id={"mp": ring_index(place + way, n)},
            device_id_type=MESH,
        )

    def arrival(step, lane):
        way = 1 if lane < SUB else -1
        owner = ring_index(place - way * (step + 1), n)
        return pltpu.make_async_remote_copy(
            src_ref=window(owner, lane),
            dst_ref=window(owner, lane),
            send_sem=send_sem.at[lane, step],
            recv_sem=recv_sem.at[lane, step],
            device_id={"mp": ring_index(place + way, n)},
            device_id_type=MESH,
        )

    order = [lane for j in range(SUB) for lane in (j, SUB + j)]
    for lane in order:
        copy(0, lane, True).start()
    me = lax.axis_index("mp")
    own = pltpu.make_async_copy(
        x_ref, out_ref.at[pl.ds(pl.multiple_of(me * rows, rows), rows)], own_sem
    )
    own.start()

    def body(step, carry):
        for lane in order:
            arrival(step - 1, lane).wait_recv()
            copy(step, lane, False).start()
        return carry

    lax.fori_loop(1, n - 1, body, 0)
    for lane in order:
        arrival(n - 2, lane).wait_recv()
        copy(0, lane, True).wait_send()

    def drain(step, carry):
        for lane in order:
            copy(step, lane, False).wait_send()
        return carry

    lax.fori_loop(1, n - 1, drain, 0)
    own.wait()


def ring_gather(x, n, collective_id):
    rows, cols = x.shape
    return pl.pallas_call(
        functools.partial(gather_kernel, n),
        out_shape=jax.ShapeDtypeStruct((n * rows, cols), x.dtype),
        in_specs=[ANY],
        out_specs=ANY,
        scratch_shapes=[
            pltpu.SemaphoreType.DMA((2 * SUB, n - 1)),
            pltpu.SemaphoreType.DMA((2 * SUB, n - 1)),
            pltpu.SemaphoreType.DMA(()),
        ],
        compiler_params=pltpu.CompilerParams(
            collective_id=collective_id, has_side_effects=True, vmem_limit_bytes=40 << 20
        ),
        name="ring_gather",
    )(x)


def scatter_kernel(n, part_ref, out_ref, held, send_sem, recv_sem):
    rows, cols = out_ref.shape
    width = cols // (2 * SUB)
    place = ring_place(lax.axis_index("mp"), n)
    greet_neighbours(place, n)

    def share(step, lane):
        way = 1 if lane < SUB else -1
        owner = ring_index(place - way * (step + 1), n)
        return part_ref.at[
            pl.ds(pl.multiple_of(owner * rows, rows), rows), pl.ds(lane * width, width)
        ]

    def copy(step, lane, first):
        way = 1 if lane < SUB else -1
        return pltpu.make_async_remote_copy(
            src_ref=share(0, lane) if first else held.at[lane, step - 1],
            dst_ref=held.at[lane, step],
            send_sem=send_sem.at[lane, step],
            recv_sem=recv_sem.at[lane, step],
            device_id={"mp": ring_index(place + way, n)},
            device_id_type=MESH,
        )

    def arrived(step, lane):
        pltpu.make_async_remote_copy(
            src_ref=held.at[lane, step],
            dst_ref=held.at[lane, step],
            send_sem=send_sem.at[lane, step],
            recv_sem=recv_sem.at[lane, step],
            device_id={"mp": ring_index(place + 1, n)},
            device_id_type=MESH,
        ).wait_recv()

    order = [lane for j in range(SUB) for lane in (j, SUB + j)]
    for lane in order:
        copy(0, lane, True).start()

    def body(step, carry):
        for lane in order:
            arrived(step - 1, lane)
            total = held[lane, step - 1].astype(jnp.float32) + share(step, lane)[...].astype(
                jnp.float32
            )
            held[lane, step - 1] = total.astype(jnp.bfloat16)
            copy(step, lane, False).start()
        return carry

    lax.fori_loop(1, n - 1, body, 0)
    for lane in order:
        arrived(n - 2, lane)
        out_ref[:, lane * width : (lane + 1) * width] = held[lane, n - 2].astype(
            jnp.float32
        ) + share(n - 1, lane)[...].astype(jnp.float32)
        copy(0, lane, True).wait_send()

    def drain(step, carry):
        for lane in order:
            copy(step, lane, False).wait_send()
        return carry

    lax.fori_loop(1, n - 1, drain, 0)


def ring_scatter(part, n, collective_id):
    rows, cols = part.shape[0] // n, part.shape[1]
    return pl.pallas_call(
        functools.partial(scatter_kernel, n),
        out_shape=jax.ShapeDtypeStruct((rows, cols), jnp.float32),
        in_specs=[VMEM],
        out_specs=VMEM,
        scratch_shapes=[
            pltpu.VMEM((2 * SUB, n - 1, rows, cols // (2 * SUB)), jnp.bfloat16),
            pltpu.SemaphoreType.DMA((2 * SUB, n - 1)),
            pltpu.SemaphoreType.DMA((2 * SUB, n - 1)),
        ],
        compiler_params=pltpu.CompilerParams(
            collective_id=collective_id, has_side_effects=True, vmem_limit_bytes=40 << 20
        ),
        name="ring_scatter",
    )(part)


def total_kernel(n, x_ref, out_ref, held, send_sem, recv_sem):
    me = lax.axis_index("mp")
    barrier = pltpu.get_barrier_semaphore()

    def greet(step, carry):
        pl.semaphore_signal(
            barrier, inc=1, device_id={"mp": lax.rem(me + step, n)}, device_id_type=MESH
        )
        return carry

    lax.fori_loop(1, n, greet, 0)
    pl.semaphore_wait(barrier, n - 1)

    def copy(step):
        return pltpu.make_async_remote_copy(
            src_ref=x_ref,
            dst_ref=held.at[step - 1],
            send_sem=send_sem.at[step - 1],
            recv_sem=recv_sem.at[step - 1],
            device_id={"mp": lax.rem(me + step, n)},
            device_id_type=MESH,
        )

    def send(step, carry):
        copy(step).start()
        return carry

    lax.fori_loop(1, n, send, 0)
    out_ref[...] = x_ref[...].astype(jnp.float32)

    def take(step, carry):
        copy(step).wait_recv()
        out_ref[...] += held[step - 1].astype(jnp.float32)
        return carry

    lax.fori_loop(1, n, take, 0)

    def drain(step, carry):
        copy(step).wait_send()
        return carry

    lax.fori_loop(1, n, drain, 0)


def small_total(x, n, collective_id):
    shape = x.shape
    x = x.reshape(-1, 128)
    total = pl.pallas_call(
        functools.partial(total_kernel, n),
        out_shape=jax.ShapeDtypeStruct(x.shape, jnp.float32),
        in_specs=[VMEM],
        out_specs=VMEM,
        scratch_shapes=[
            pltpu.VMEM((n - 1,) + x.shape, x.dtype),
            pltpu.SemaphoreType.DMA((n - 1,)),
            pltpu.SemaphoreType.DMA((n - 1,)),
        ],
        compiler_params=pltpu.CompilerParams(collective_id=collective_id, has_side_effects=True),
        name="small_total",
    )(x)
    return total.astype(jnp.bfloat16).reshape(shape)


def pick_kernel(count, index_ref, table_ref, out_ref, sems):
    def copy(i):
        return pltpu.make_async_copy(table_ref.at[index_ref[i]], out_ref.at[i], sems.at[i])

    for i in range(count):
        copy(i).start()
    for i in range(count):
        copy(i).wait()


def pick(table, index):
    count = index.shape[0]
    return pl.pallas_call(
        functools.partial(pick_kernel, count),
        out_shape=jax.ShapeDtypeStruct((count,) + table.shape[1:], table.dtype),
        in_specs=[SMEM, ANY],
        out_specs=ANY,
        scratch_shapes=[pltpu.SemaphoreType.DMA((count,))],
        compiler_params=pltpu.CompilerParams(vmem_limit_bytes=40 << 20),
        name="pick",
    )(index, table)


def permuted_gather(x, n):
    rows, cols = x.shape
    place = ring_place(lax.axis_index("mp"), n)
    index = [2 * p if p < n // 2 else 2 * (n - 1 - p) + 1 for p in range(n)]
    pairs = {
        way: [(index[p], index[(p + way) % n]) for p in range(n)] for way in (1, -1)
    }
    parts = [(lax.axis_index("mp"), x)]
    for way, steps in ((1, n // 2), (-1, n - 1 - n // 2)):
        held = x
        for step in range(1, steps + 1):
            held = lax.ppermute(held, "mp", pairs[way])
            parts.append((ring_index(place - way * step, n), held))
    out = jnp.zeros((n * rows, cols), x.dtype)
    for owner, part in parts:
        out = lax.dynamic_update_slice(out, part, (owner * rows, 0))
    return out


def rms_scale(values, scaling):
    mean_square = jnp.mean(values * values, axis=-1, keepdims=True)
    return values * lax.rsqrt(mean_square + EPS) * scaling


def apply_rotary(values, token_positions):
    half_dim = values.shape[-1] // 2
    frequency = 10000.0 ** (-2.0 * jnp.arange(half_dim, dtype=jnp.float32) / values.shape[-1])
    angles = token_positions.astype(jnp.float32)[:, None] * frequency[None, :]
    cosine = jnp.cos(angles)[:, None, :]
    sine_part = jnp.sin(angles)[:, None, :]
    first_half = values[..., :half_dim]
    second_half = values[..., half_dim:]
    return jnp.concatenate(
        [
            first_half * cosine - second_half * sine_part,
            second_half * cosine + first_half * sine_part,
        ],
        axis=-1,
    )


def positions_of(segments):
    length = segments.shape[0]
    earlier = jnp.sum((segments[None, :] < segments[:, None]).astype(jnp.int32), axis=1)
    return PPR * PAGE + jnp.arange(length, dtype=jnp.int32) - earlier


def capped(scores):
    return SOFTCAP * jnp.tanh(scores / SOFTCAP)


def attend_local(query_rows, keys_new, fresh_values, keys_pre, values_pre, segments):
    scale_factor = 1.0 / math.sqrt(HIDDEN_BREADTH // ASKING_CHANNELS)
    length = segments.shape[0]
    prefix_owner = jnp.arange(keys_pre.shape[1], dtype=jnp.int32) // (PPR * PAGE)
    mask_pre = (prefix_owner[None, :] == segments[:, None])[None]
    ordinal = jnp.arange(length, dtype=jnp.int32)
    mask_new = ((segments[None, :] == segments[:, None]) & (ordinal[None, :] <= ordinal[:, None]))[
        None
    ]
    scores_pre = (
        jnp.einsum("thd,hjd->htj", query_rows, keys_pre, preferred_element_type=jnp.float32)
        * scale_factor
    )
    scores_new = (
        jnp.einsum("thd,uhd->htu", query_rows, keys_new, preferred_element_type=jnp.float32)
        * scale_factor
    )
    weight_pre = jnp.where(mask_pre, jnp.exp(capped(scores_pre)), 0.0)
    weight_new = jnp.where(mask_new, jnp.exp(capped(scores_new)), 0.0)
    totals = jnp.sum(weight_pre, axis=-1, keepdims=True) + jnp.sum(
        weight_new, axis=-1, keepdims=True
    )
    probs_pre = (weight_pre / totals).astype(jnp.bfloat16)
    probs_new = (weight_new / totals).astype(jnp.bfloat16)
    mixture = jnp.einsum("htj,hjd->thd", probs_pre, values_pre, preferred_element_type=jnp.float32)
    mixture = mixture + jnp.einsum(
        "htu,uhd->thd", probs_new, fresh_values, preferred_element_type=jnp.float32
    )
    return mixture.astype(jnp.bfloat16).reshape(length, -1)


def shards(
    residual_input,
    before_attention_gain,
    after_attention_gain,
    before_feedforward_gain,
    after_feedforward_gain,
    query_weight,
    key_value_weight,
    output_weight,
    gate_matrix,
    up_matrix,
    down_matrix,
    key_value_cache,
    projected_lowrank_left,
    projected_lowrank_right,
    result_lowrank_left,
    result_lowrank_right,
    token_request,
    lowrank_choice_by_prompt,
    adapter_position,
    request_pages,
):
    mp_index = lax.axis_index("mp")
    dp_index = lax.axis_index("dp")
    residual = residual_input.astype(jnp.float32)
    normed_rows = rms_scale(residual, before_attention_gain).astype(jnp.bfloat16)
    n_mp = lax.axis_size("mp")
    normalized_rows = permuted_gather(normed_rows, n_mp)
    prompt_ordinal = normalized_rows.shape[0]
    channel_window = query_weight.shape[1] // CHANNEL_LENGTH
    query_rows = jnp.dot(normalized_rows, query_weight, preferred_element_type=jnp.float32).reshape(
        prompt_ordinal, channel_window, CHANNEL_LENGTH
    )
    shared = 2 if channel_window % 2 == 0 else 1
    pair_window = channel_window // shared
    key_value_rows = jnp.dot(
        normalized_rows,
        key_value_weight[:, :, ::shared].reshape(HIDDEN_BREADTH, 2 * pair_window * CHANNEL_LENGTH),
        preferred_element_type=jnp.float32,
    ).reshape(prompt_ordinal, 2, pair_window, CHANNEL_LENGTH)
    segments = token_request[0]
    request_ids = lowrank_choice_by_prompt[0]
    request_range = jnp.arange(SHARD_PROMPTS, dtype=jnp.int32)
    membership = segments[:, None] == request_range[None, :]
    adapter_range = jnp.arange(NUM_LOW_TERMS, dtype=jnp.int32)
    token_adapter = jnp.sum(jnp.where(membership, request_ids[None, :], 0), axis=1)
    token_adapter_slot = jnp.sum(
        jnp.where(token_adapter[:, None] == adapter_range[None, :], adapter_position[None, :], 0),
        axis=1,
    )
    slot_count = projected_lowrank_left.shape[0]
    own_slots = mp_index * slot_count + jnp.arange(slot_count, dtype=jnp.int32)
    resident_here = token_adapter_slot[:, None] == own_slots[None, :]
    slot_factors = jnp.dot(
        normalized_rows,
        jnp.transpose(projected_lowrank_left, (1, 0, 2)).reshape(
            HIDDEN_BREADTH, slot_count * LOW_DIMENSION
        ),
        preferred_element_type=jnp.float32,
    ).reshape(prompt_ordinal, slot_count, LOW_DIMENSION)
    lowrank_source = small_total(
        jnp.sum(jnp.where(resident_here[:, :, None], slot_factors, 0.0), axis=1).astype(
            jnp.bfloat16
        ),
        n_mp,
        3,
    )
    choice_mask_table = membership.astype(jnp.bfloat16)
    broadened_lines = (choice_mask_table[:, :, None] * lowrank_source[:, None, :]).reshape(
        prompt_ordinal, SHARD_PROMPTS * LOW_DIMENSION
    )
    raised_result_lines = pick(projected_lowrank_right, request_ids).reshape(
        SHARD_PROMPTS * LOW_DIMENSION, 3 * channel_window * CHANNEL_LENGTH
    )
    adapter_query_key_value = jnp.dot(
        broadened_lines, raised_result_lines, preferred_element_type=jnp.float32
    ).reshape(prompt_ordinal, 3, channel_window, CHANNEL_LENGTH)
    token_positions = positions_of(segments)
    rotary_queries = apply_rotary(
        query_rows + adapter_query_key_value[:, 0], token_positions
    ).astype(jnp.bfloat16)
    rotary_keys = apply_rotary(
        key_value_rows[:, 0] + adapter_query_key_value[:, 1, ::shared], token_positions
    ).astype(jnp.bfloat16)
    fresh_values = (key_value_rows[:, 1] + adapter_query_key_value[:, 2, ::shared]).astype(
        jnp.bfloat16
    )
    rotary_keys = jnp.repeat(rotary_keys, shared, axis=1)
    fresh_values = jnp.repeat(fresh_values, shared, axis=1)
    kv_new = jnp.stack([rotary_keys, fresh_values], axis=1)
    own_pages = lax.dynamic_index_in_dim(request_pages, dp_index, 0, keepdims=False).reshape(
        SHARD_PROMPTS * PPR
    )
    whole_pool = lax.all_gather(key_value_cache[:, :, ::shared], "dp", axis=0, tiled=True)
    chosen = pick(whole_pool, own_pages)
    prefix = jnp.repeat(
        jnp.transpose(chosen, (1, 2, 0, 3, 4)).reshape(
            2, pair_window, SHARD_PROMPTS * PPR * PAGE, CHANNEL_LENGTH
        ),
        shared,
        axis=1,
    )
    keys_pre, values_pre = prefix[0], prefix[1]
    attended = attend_local(
        rotary_queries, rotary_keys, fresh_values, keys_pre, values_pre, segments
    )
    request_output_down = pick(result_lowrank_left, request_ids)
    request_output_factors = jnp.einsum(
        "tc,rck->trk", attended, request_output_down, preferred_element_type=jnp.float32
    )
    output_adapter_piece = jnp.sum(
        jnp.where(membership[:, :, None], request_output_factors, 0.0), axis=1
    )
    result_lowrank_source = small_total(output_adapter_piece.astype(jnp.bfloat16), n_mp, 4)
    result_seat_lines = result_lowrank_right.shape[0]
    broadened_result = (resident_here.astype(jnp.bfloat16)[:, :, None] * result_lowrank_source[:, None, :]).reshape(
        prompt_ordinal, result_seat_lines * LOW_DIMENSION
    )
    raised_window = result_lowrank_right.reshape(result_seat_lines * LOW_DIMENSION, HIDDEN_BREADTH)
    attn_sum = ring_scatter(
        (
            jnp.dot(attended, output_weight, preferred_element_type=jnp.float32)
            + jnp.dot(broadened_result, raised_window, preferred_element_type=jnp.float32)
        ).astype(jnp.bfloat16),
        n_mp,
        1,
    )
    after_attn = (residual + rms_scale(attn_sum, after_attention_gain)).astype(jnp.bfloat16)
    normed_ffw = rms_scale(after_attn.astype(jnp.float32), before_feedforward_gain).astype(
        jnp.bfloat16
    )
    piece = ring_gather(normed_ffw, n_mp, 0)
    gated = jnp.dot(piece, gate_matrix, preferred_element_type=jnp.float32)
    upward = jnp.dot(piece, up_matrix, preferred_element_type=jnp.float32)
    hidden = (jax.nn.gelu(gated, approximate=True) * upward).astype(jnp.bfloat16)
    ffw_sum = ring_scatter(
        jnp.dot(hidden, down_matrix, preferred_element_type=jnp.float32).astype(jnp.bfloat16),
        n_mp,
        2,
    )
    hidden_out = (
        after_attn.astype(jnp.float32) + rms_scale(ffw_sum, after_feedforward_gain)
    ).astype(jnp.bfloat16)
    return (hidden_out, kv_new)


def solution(mesh):
    return jax.shard_map(
        shards,
        mesh=mesh,
        in_specs=(
            P(("dp", "mp"), None),
            P(),
            P(),
            P(),
            P(),
            P(None, "mp"),
            P(None, None, "mp", None),
            P("mp", None),
            P(None, "mp"),
            P(None, "mp"),
            P("mp", None),
            P("dp", None, "mp", None, None),
            P("mp", None, None),
            P(None, None, None, "mp", None),
            P(None, "mp", None),
            P("mp", None, None),
            P("dp", None),
            P("dp", None),
            P(),
            P(),
        ),
        out_specs=(P(("dp", "mp"), None), P("dp", None, "mp", None)),
        check_vma=False,
    )
```

```python
import functools
import math

import jax
import jax.numpy as jnp
from jax import lax
from jax.experimental import pallas as pl
from jax.experimental.pallas import tpu as pltpu
from jax.sharding import PartitionSpec as P

HIDDEN_BREADTH = 4608
ASKING_CHANNELS = 32
CHANNEL_LENGTH = 128
NUM_LOW_TERMS = 64
LOW_DIMENSION = 16
SHARD_PROMPTS = 8
PPR = 4
PAGE = 16


EPS = 1e-06
SOFTCAP = 50.0
MESH = pl.DeviceIdType.MESH
ANY = pl.BlockSpec(memory_space=pl.ANY)
VMEM = pl.BlockSpec(memory_space=pltpu.VMEM)
SMEM = pl.BlockSpec(memory_space=pltpu.SMEM)


def ring_place(index, n):
    return jnp.where(index % 2 == 0, index // 2, n - 1 - index // 2)


def ring_index(place, n):
    place = lax.rem(place + 2 * n, n)
    return jnp.where(place < n // 2, 2 * place, 2 * (n - 1 - place) + 1)


def greet_neighbours(place, n):
    barrier = pltpu.get_barrier_semaphore()
    for way in (1, -1):
        pl.semaphore_signal(
            barrier, inc=1, device_id={"mp": ring_index(place + way, n)}, device_id_type=MESH
        )
    pl.semaphore_wait(barrier, 2)


SUB = 2


def gather_kernel(n, x_ref, out_ref, send_sem, recv_sem, own_sem):
    rows, cols = x_ref.shape
    width = cols // (2 * SUB)
    place = ring_place(lax.axis_index("mp"), n)
    greet_neighbours(place, n)

    def window(owner, lane):
        return out_ref.at[
            pl.ds(pl.multiple_of(owner * rows, rows), rows), pl.ds(lane * width, width)
        ]

    def copy(step, lane, first):
        way = 1 if lane < SUB else -1
        owner = ring_index(place - way * step, n)
        src = x_ref.at[:, pl.ds(lane * width, width)] if first else window(owner, lane)
        return pltpu.make_async_remote_copy(
            src_ref=src,
            dst_ref=window(owner, lane),
            send_sem=send_sem.at[lane, step],
            recv_sem=recv_sem.at[lane, step],
            device_id={"mp": ring_index(place + way, n)},
            device_id_type=MESH,
        )

    def arrival(step, lane):
        way = 1 if lane < SUB else -1
        owner = ring_index(place - way * (step + 1), n)
        return pltpu.make_async_remote_copy(
            src_ref=window(owner, lane),
            dst_ref=window(owner, lane),
            send_sem=send_sem.at[lane, step],
            recv_sem=recv_sem.at[lane, step],
            device_id={"mp": ring_index(place + way, n)},
            device_id_type=MESH,
        )

    order = [lane for j in range(SUB) for lane in (j, SUB + j)]
    for lane in order:
        copy(0, lane, True).start()
    me = lax.axis_index("mp")
    own = pltpu.make_async_copy(
        x_ref, out_ref.at[pl.ds(pl.multiple_of(me * rows, rows), rows)], own_sem
    )
    own.start()

    def body(step, carry):
        for lane in order:
            arrival(step - 1, lane).wait_recv()
            copy(step, lane, False).start()
        return carry

    lax.fori_loop(1, n - 1, body, 0)
    for lane in order:
        arrival(n - 2, lane).wait_recv()
        copy(0, lane, True).wait_send()

    def drain(step, carry):
        for lane in order:
            copy(step, lane, False).wait_send()
        return carry

    lax.fori_loop(1, n - 1, drain, 0)
    own.wait()


def ring_gather(x, n, collective_id):
    rows, cols = x.shape
    return pl.pallas_call(
        functools.partial(gather_kernel, n),
        out_shape=jax.ShapeDtypeStruct((n * rows, cols), x.dtype),
        in_specs=[ANY],
        out_specs=ANY,
        scratch_shapes=[
            pltpu.SemaphoreType.DMA((2 * SUB, n - 1)),
            pltpu.SemaphoreType.DMA((2 * SUB, n - 1)),
            pltpu.SemaphoreType.DMA(()),
        ],
        compiler_params=pltpu.CompilerParams(
            collective_id=collective_id, has_side_effects=True, vmem_limit_bytes=40 << 20
        ),
        name="ring_gather",
    )(x)


def scatter_kernel(n, part_ref, out_ref, held, send_sem, recv_sem):
    rows, cols = out_ref.shape
    width = cols // (2 * SUB)
    place = ring_place(lax.axis_index("mp"), n)
    greet_neighbours(place, n)

    def share(step, lane):
        way = 1 if lane < SUB else -1
        owner = ring_index(place - way * (step + 1), n)
        return part_ref.at[
            pl.ds(pl.multiple_of(owner * rows, rows), rows), pl.ds(lane * width, width)
        ]

    def copy(step, lane, first):
        way = 1 if lane < SUB else -1
        return pltpu.make_async_remote_copy(
            src_ref=share(0, lane) if first else held.at[lane, step - 1],
            dst_ref=held.at[lane, step],
            send_sem=send_sem.at[lane, step],
            recv_sem=recv_sem.at[lane, step],
            device_id={"mp": ring_index(place + way, n)},
            device_id_type=MESH,
        )

    def arrived(step, lane):
        pltpu.make_async_remote_copy(
            src_ref=held.at[lane, step],
            dst_ref=held.at[lane, step],
            send_sem=send_sem.at[lane, step],
            recv_sem=recv_sem.at[lane, step],
            device_id={"mp": ring_index(place + 1, n)},
            device_id_type=MESH,
        ).wait_recv()

    order = [lane for j in range(SUB) for lane in (j, SUB + j)]
    for lane in order:
        copy(0, lane, True).start()

    def body(step, carry):
        for lane in order:
            arrived(step - 1, lane)
            total = held[lane, step - 1].astype(jnp.float32) + share(step, lane)[...].astype(
                jnp.float32
            )
            held[lane, step - 1] = total.astype(jnp.bfloat16)
            copy(step, lane, False).start()
        return carry

    lax.fori_loop(1, n - 1, body, 0)
    for lane in order:
        arrived(n - 2, lane)
        out_ref[:, lane * width : (lane + 1) * width] = held[lane, n - 2].astype(
            jnp.float32
        ) + share(n - 1, lane)[...].astype(jnp.float32)
        copy(0, lane, True).wait_send()

    def drain(step, carry):
        for lane in order:
            copy(step, lane, False).wait_send()
        return carry

    lax.fori_loop(1, n - 1, drain, 0)


def ring_scatter(part, n, collective_id):
    rows, cols = part.shape[0] // n, part.shape[1]
    return pl.pallas_call(
        functools.partial(scatter_kernel, n),
        out_shape=jax.ShapeDtypeStruct((rows, cols), jnp.float32),
        in_specs=[VMEM],
        out_specs=VMEM,
        scratch_shapes=[
            pltpu.VMEM((2 * SUB, n - 1, rows, cols // (2 * SUB)), jnp.bfloat16),
            pltpu.SemaphoreType.DMA((2 * SUB, n - 1)),
            pltpu.SemaphoreType.DMA((2 * SUB, n - 1)),
        ],
        compiler_params=pltpu.CompilerParams(
            collective_id=collective_id, has_side_effects=True, vmem_limit_bytes=40 << 20
        ),
        name="ring_scatter",
    )(part)


def total_kernel(n, x_ref, out_ref, held, send_sem, recv_sem):
    me = lax.axis_index("mp")
    barrier = pltpu.get_barrier_semaphore()

    def greet(step, carry):
        pl.semaphore_signal(
            barrier, inc=1, device_id={"mp": lax.rem(me + step, n)}, device_id_type=MESH
        )
        return carry

    lax.fori_loop(1, n, greet, 0)
    pl.semaphore_wait(barrier, n - 1)

    def copy(step):
        return pltpu.make_async_remote_copy(
            src_ref=x_ref,
            dst_ref=held.at[step - 1],
            send_sem=send_sem.at[step - 1],
            recv_sem=recv_sem.at[step - 1],
            device_id={"mp": lax.rem(me + step, n)},
            device_id_type=MESH,
        )

    def send(step, carry):
        copy(step).start()
        return carry

    lax.fori_loop(1, n, send, 0)
    out_ref[...] = x_ref[...].astype(jnp.float32)

    def take(step, carry):
        copy(step).wait_recv()
        out_ref[...] += held[step - 1].astype(jnp.float32)
        return carry

    lax.fori_loop(1, n, take, 0)

    def drain(step, carry):
        copy(step).wait_send()
        return carry

    lax.fori_loop(1, n, drain, 0)


def small_total(x, n, collective_id):
    shape = x.shape
    x = x.reshape(-1, 128)
    total = pl.pallas_call(
        functools.partial(total_kernel, n),
        out_shape=jax.ShapeDtypeStruct(x.shape, jnp.float32),
        in_specs=[VMEM],
        out_specs=VMEM,
        scratch_shapes=[
            pltpu.VMEM((n - 1,) + x.shape, x.dtype),
            pltpu.SemaphoreType.DMA((n - 1,)),
            pltpu.SemaphoreType.DMA((n - 1,)),
        ],
        compiler_params=pltpu.CompilerParams(collective_id=collective_id, has_side_effects=True),
        name="small_total",
    )(x)
    return total.astype(jnp.bfloat16).reshape(shape)


def pick_kernel(count, index_ref, table_ref, out_ref, sems):
    def copy(i):
        return pltpu.make_async_copy(table_ref.at[index_ref[i]], out_ref.at[i], sems.at[i])

    for i in range(count):
        copy(i).start()
    for i in range(count):
        copy(i).wait()


def pick(table, index):
    count = index.shape[0]
    return pl.pallas_call(
        functools.partial(pick_kernel, count),
        out_shape=jax.ShapeDtypeStruct((count,) + table.shape[1:], table.dtype),
        in_specs=[SMEM, ANY],
        out_specs=ANY,
        scratch_shapes=[pltpu.SemaphoreType.DMA((count,))],
        compiler_params=pltpu.CompilerParams(vmem_limit_bytes=40 << 20),
        name="pick",
    )(index, table)


def permuted_gather(x, n):
    rows, cols = x.shape
    place = ring_place(lax.axis_index("mp"), n)
    index = [2 * p if p < n // 2 else 2 * (n - 1 - p) + 1 for p in range(n)]
    pairs = {
        way: [(index[p], index[(p + way) % n]) for p in range(n)] for way in (1, -1)
    }
    parts = [(lax.axis_index("mp"), x)]
    for way, steps in ((1, n // 2), (-1, n - 1 - n // 2)):
        held = x
        for step in range(1, steps + 1):
            held = lax.ppermute(held, "mp", pairs[way])
            parts.append((ring_index(place - way * step, n), held))
    out = jnp.zeros((n * rows, cols), x.dtype)
    for owner, part in parts:
        out = lax.dynamic_update_slice(out, part, (owner * rows, 0))
    return out


def rms_scale(values, scaling):
    mean_square = jnp.mean(values * values, axis=-1, keepdims=True)
    return values * lax.rsqrt(mean_square + EPS) * scaling


def apply_rotary(values, token_positions):
    half_dim = values.shape[-1] // 2
    frequency = 10000.0 ** (-2.0 * jnp.arange(half_dim, dtype=jnp.float32) / values.shape[-1])
    angles = token_positions.astype(jnp.float32)[:, None] * frequency[None, :]
    cosine = jnp.cos(angles)[:, None, :]
    sine_part = jnp.sin(angles)[:, None, :]
    first_half = values[..., :half_dim]
    second_half = values[..., half_dim:]
    return jnp.concatenate(
        [
            first_half * cosine - second_half * sine_part,
            second_half * cosine + first_half * sine_part,
        ],
        axis=-1,
    )


def positions_of(segments):
    length = segments.shape[0]
    earlier = jnp.sum((segments[None, :] < segments[:, None]).astype(jnp.int32), axis=1)
    return PPR * PAGE + jnp.arange(length, dtype=jnp.int32) - earlier


def capped(scores):
    return SOFTCAP * jnp.tanh(scores / SOFTCAP)


def attend_local(query_rows, keys_new, fresh_values, keys_pre, values_pre, segments):
    scale_factor = 1.0 / math.sqrt(HIDDEN_BREADTH // ASKING_CHANNELS)
    length = segments.shape[0]
    prefix_owner = jnp.arange(keys_pre.shape[1], dtype=jnp.int32) // (PPR * PAGE)
    mask_pre = (prefix_owner[None, :] == segments[:, None])[None]
    ordinal = jnp.arange(length, dtype=jnp.int32)
    mask_new = ((segments[None, :] == segments[:, None]) & (ordinal[None, :] <= ordinal[:, None]))[
        None
    ]
    scores_pre = (
        jnp.einsum("thd,hjd->htj", query_rows, keys_pre, preferred_element_type=jnp.float32)
        * scale_factor
    )
    scores_new = (
        jnp.einsum("thd,uhd->htu", query_rows, keys_new, preferred_element_type=jnp.float32)
        * scale_factor
    )
    weight_pre = jnp.where(mask_pre, jnp.exp(capped(scores_pre)), 0.0)
    weight_new = jnp.where(mask_new, jnp.exp(capped(scores_new)), 0.0)
    totals = jnp.sum(weight_pre, axis=-1, keepdims=True) + jnp.sum(
        weight_new, axis=-1, keepdims=True
    )
    probs_pre = (weight_pre / totals).astype(jnp.bfloat16)
    probs_new = (weight_new / totals).astype(jnp.bfloat16)
    mixture = jnp.einsum("htj,hjd->thd", probs_pre, values_pre, preferred_element_type=jnp.float32)
    mixture = mixture + jnp.einsum(
        "htu,uhd->thd", probs_new, fresh_values, preferred_element_type=jnp.float32
    )
    return mixture.astype(jnp.bfloat16).reshape(length, -1)


def shards(
    residual_input,
    before_attention_gain,
    after_attention_gain,
    before_feedforward_gain,
    after_feedforward_gain,
    query_weight,
    key_value_weight,
    output_weight,
    gate_matrix,
    up_matrix,
    down_matrix,
    key_value_cache,
    projected_lowrank_left,
    projected_lowrank_right,
    result_lowrank_left,
    result_lowrank_right,
    token_request,
    lowrank_choice_by_prompt,
    adapter_position,
    request_pages,
):
    mp_index = lax.axis_index("mp")
    dp_index = lax.axis_index("dp")
    residual = residual_input.astype(jnp.float32)
    normed_rows = rms_scale(residual, before_attention_gain).astype(jnp.bfloat16)
    n_mp = lax.axis_size("mp")
    normalized_rows = permuted_gather(normed_rows, n_mp)
    prompt_ordinal = normalized_rows.shape[0]
    channel_window = query_weight.shape[1] // CHANNEL_LENGTH
    query_rows = jnp.dot(normalized_rows, query_weight, preferred_element_type=jnp.float32).reshape(
        prompt_ordinal, channel_window, CHANNEL_LENGTH
    )
    shared = 2 if channel_window % 2 == 0 else 1
    pair_window = channel_window // shared
    key_value_rows = jnp.dot(
        normalized_rows,
        key_value_weight.reshape(HIDDEN_BREADTH, 2 * channel_window * CHANNEL_LENGTH),
        preferred_element_type=jnp.float32,
    ).reshape(prompt_ordinal, 2, channel_window, CHANNEL_LENGTH)
    segments = token_request[0]
    request_ids = lowrank_choice_by_prompt[0]
    request_range = jnp.arange(SHARD_PROMPTS, dtype=jnp.int32)
    membership = segments[:, None] == request_range[None, :]
    adapter_range = jnp.arange(NUM_LOW_TERMS, dtype=jnp.int32)
    token_adapter = jnp.sum(jnp.where(membership, request_ids[None, :], 0), axis=1)
    token_adapter_slot = jnp.sum(
        jnp.where(token_adapter[:, None] == adapter_range[None, :], adapter_position[None, :], 0),
        axis=1,
    )
    slot_count = projected_lowrank_left.shape[0]
    own_slots = mp_index * slot_count + jnp.arange(slot_count, dtype=jnp.int32)
    resident_here = token_adapter_slot[:, None] == own_slots[None, :]
    slot_factors = jnp.dot(
        normalized_rows,
        jnp.transpose(projected_lowrank_left, (1, 0, 2)).reshape(
            HIDDEN_BREADTH, slot_count * LOW_DIMENSION
        ),
        preferred_element_type=jnp.float32,
    ).reshape(prompt_ordinal, slot_count, LOW_DIMENSION)
    lowrank_source = small_total(
        jnp.sum(jnp.where(resident_here[:, :, None], slot_factors, 0.0), axis=1).astype(
            jnp.bfloat16
        ),
        n_mp,
        3,
    )
    choice_mask_table = membership.astype(jnp.bfloat16)
    broadened_lines = (choice_mask_table[:, :, None] * lowrank_source[:, None, :]).reshape(
        prompt_ordinal, SHARD_PROMPTS * LOW_DIMENSION
    )
    raised_result_lines = pick(projected_lowrank_right, request_ids).reshape(
        SHARD_PROMPTS * LOW_DIMENSION, 3 * channel_window * CHANNEL_LENGTH
    )
    adapter_query_key_value = jnp.dot(
        broadened_lines, raised_result_lines, preferred_element_type=jnp.float32
    ).reshape(prompt_ordinal, 3, channel_window, CHANNEL_LENGTH)
    token_positions = positions_of(segments)
    rotary_queries = apply_rotary(
        query_rows + adapter_query_key_value[:, 0], token_positions
    ).astype(jnp.bfloat16)
    rotary_keys = apply_rotary(
        key_value_rows[:, 0] + adapter_query_key_value[:, 1], token_positions
    ).astype(jnp.bfloat16)
    fresh_values = (key_value_rows[:, 1] + adapter_query_key_value[:, 2]).astype(
        jnp.bfloat16
    )
    kv_new = jnp.stack([rotary_keys, fresh_values], axis=1)
    own_pages = lax.dynamic_index_in_dim(request_pages, dp_index, 0, keepdims=False).reshape(
        SHARD_PROMPTS * PPR
    )
    whole_pool = lax.all_gather(key_value_cache[:, :, ::shared], "dp", axis=0, tiled=True)
    chosen = pick(whole_pool, own_pages)
    prefix = jnp.repeat(
        jnp.transpose(chosen, (1, 2, 0, 3, 4)).reshape(
            2, pair_window, SHARD_PROMPTS * PPR * PAGE, CHANNEL_LENGTH
        ),
        shared,
        axis=1,
    )
    keys_pre, values_pre = prefix[0], prefix[1]
    attended = attend_local(
        rotary_queries, rotary_keys, fresh_values, keys_pre, values_pre, segments
    )
    request_output_down = pick(result_lowrank_left, request_ids)
    request_output_factors = jnp.einsum(
        "tc,rck->trk", attended, request_output_down, preferred_element_type=jnp.float32
    )
    output_adapter_piece = jnp.sum(
        jnp.where(membership[:, :, None], request_output_factors, 0.0), axis=1
    )
    result_lowrank_source = small_total(output_adapter_piece.astype(jnp.bfloat16), n_mp, 4)
    result_seat_lines = result_lowrank_right.shape[0]
    broadened_result = (resident_here.astype(jnp.bfloat16)[:, :, None] * result_lowrank_source[:, None, :]).reshape(
        prompt_ordinal, result_seat_lines * LOW_DIMENSION
    )
    raised_window = result_lowrank_right.reshape(result_seat_lines * LOW_DIMENSION, HIDDEN_BREADTH)
    attn_sum = ring_scatter(
        (
            jnp.dot(attended, output_weight, preferred_element_type=jnp.float32)
            + jnp.dot(broadened_result, raised_window, preferred_element_type=jnp.float32)
        ).astype(jnp.bfloat16),
        n_mp,
        1,
    )
    after_attn = (residual + rms_scale(attn_sum, after_attention_gain)).astype(jnp.bfloat16)
    normed_ffw = rms_scale(after_attn.astype(jnp.float32), before_feedforward_gain).astype(
        jnp.bfloat16
    )
    piece = ring_gather(normed_ffw, n_mp, 0)
    gated = jnp.dot(piece, gate_matrix, preferred_element_type=jnp.float32)
    upward = jnp.dot(piece, up_matrix, preferred_element_type=jnp.float32)
    hidden = (jax.nn.gelu(gated, approximate=True) * upward).astype(jnp.bfloat16)
    ffw_sum = ring_scatter(
        jnp.dot(hidden, down_matrix, preferred_element_type=jnp.float32).astype(jnp.bfloat16),
        n_mp,
        2,
    )
    hidden_out = (
        after_attn.astype(jnp.float32) + rms_scale(ffw_sum, after_feedforward_gain)
    ).astype(jnp.bfloat16)
    return (hidden_out, kv_new)


def solution(mesh):
    return jax.shard_map(
        shards,
        mesh=mesh,
        in_specs=(
            P(("dp", "mp"), None),
            P(),
            P(),
            P(),
            P(),
            P(None, "mp"),
            P(None, None, "mp", None),
            P("mp", None),
            P(None, "mp"),
            P(None, "mp"),
            P("mp", None),
            P("dp", None, "mp", None, None),
            P("mp", None, None),
            P(None, None, None, "mp", None),
            P(None, "mp", None),
            P("mp", None, None),
            P("dp", None),
            P("dp", None),
            P(),
            P(),
        ),
        out_specs=(P(("dp", "mp"), None), P("dp", None, "mp", None)),
        check_vma=False,
    )
```
